128 devices in a mesh: group: 8 (over x, core), local: 16 (over y, z).
Axes of the slice: x: 4, y: 4, z: 4, core: 2. Of those that a mesh axis runs over, the one named last changes fastest.
Arguments:
- tokens: bfloat16 [2048, 3584], P(('group', 'local')), may hold values from -6 to 6
- out_grad: bfloat16 [2048, 3584], P(('group', 'local')), may hold values from -6 to 6
- expert_ids: int32 [2048, 8], P(('group', 'local')), may hold values from 0 to 127, as said below
- probs: bfloat16 [2048, 8], P(('group', 'local')), may hold values from 0.049804688 to 0.3984375
- w_gate: bfloat16 [128, 3584, 1024], P(('group', 'local')), may hold values from -0.09375 to 0.09375
- w_up: bfloat16 [128, 3584, 1024], P(('group', 'local')), may hold values from -0.09375 to 0.09375
- w_down: bfloat16 [128, 1024, 3584], P(('group', 'local')), may hold values from -0.1875 to 0.1875
Outputs:
- d_tokens: bfloat16 [2048, 3584], P(('group', 'local'))
The draws below stay inside these ranges and needn't reach their ends.
Inputs may be any that keep to these rules, and one draw needn't show every extreme that they name: `expert_ids`: each token names 8 different experts, 2 in each of 4 node groups, expert e lying in node group e // 16. One node group, drawn from the seed, is chosen by every token. Within the tokens of one device the experts of one node group are named equally often, up to one, so that no expert is named more than 2 times by the tokens of one device; the experts of the common node group reach 2 on every device.
All inputs are finite; a program needn't handle non-finite values.
Results may differ from the reference program's by a relative error of at most 0.012.
Values may be sent and summed in bfloat16 or wider, within the bound.
A program may use at most 128 MiB of HBM per device.

```python
import jax
import jax.numpy as jnp
from jax import lax

D = 3584
F = 1024
TOP = 8
GROUPS_TOKEN = 4
TOK_DEV = 16
GROUPS = 8
GROUP_EXPERTS = 16
EXPERTS = 128
CAP = 2
TOKENS = 2048


def draw_expert_ids(key, part):
    key = jax.random.fold_in(key, 11)
    keys = jax.random.split(key, 3)
    blocks = TOKENS // TOK_DEV
    per_group = TOP // GROUPS_TOKEN
    group_list = jnp.arange(GROUPS, dtype=jnp.int32)
    common = jax.random.randint(keys[0], (), 0, GROUPS)
    scores = jax.random.randint(keys[1], (blocks, TOK_DEV, GROUPS), 0, 1 << 20) * GROUPS + group_list
    scores = scores + jnp.where(group_list == common, 1 << 26, 0)
    chosen = lax.top_k(scores, GROUPS_TOKEN)[1].astype(jnp.int32)
    member = jnp.any(chosen[..., None] == group_list, axis=2).astype(jnp.int32)
    ranking = jnp.cumsum(member, axis=1) - member
    order_scores = jax.random.randint(keys[2], (blocks, GROUPS, GROUP_EXPERTS), 0, 1 << 20) * GROUP_EXPERTS
    order_scores = order_scores + jnp.arange(GROUP_EXPERTS, dtype=jnp.int32)
    shuffle = jnp.argsort(order_scores, axis=-1).astype(jnp.int32).reshape(-1)
    chosen_rank = jnp.take_along_axis(ranking, chosen, axis=2)
    offsets = jnp.arange(per_group, dtype=jnp.int32)
    position = (per_group * chosen_rank[..., None] + offsets) % GROUP_EXPERTS
    block_list = jnp.arange(blocks, dtype=jnp.int32)[:, None, None, None]
    flat_index = (block_list * GROUPS + chosen[..., None]) * GROUP_EXPERTS + position
    local_expert = shuffle[flat_index]
    result = chosen[..., None] * GROUP_EXPERTS + local_expert
    return result.reshape(TOKENS, TOP).astype(jnp.int32)


def steps_of(own_key, dims, cuts, smallest, high):
    gain, own = 1.0, jax.random.fold_in(own_key, 6)
    for axis_at, parts in cuts:
        steps = jnp.exp(jax.random.uniform(jax.random.fold_in(own, axis_at), (parts,), jnp.float32, smallest / len(cuts), high / len(cuts)))
        gain = gain * jnp.repeat(steps, dims[axis_at] // parts).reshape([-1 if axis == axis_at else 1 for axis in range(len(dims))])
    return gain


def noise(stream_key, extent, deviation, bound, pieces=(), held_as=jnp.bfloat16):
    values = jax.random.normal(stream_key, extent, jnp.float32) * deviation
    if len(pieces) > 0:
        values = steps_of(stream_key, extent, pieces, -0.22, 0.18) * values
    return jnp.clip(values, min=-bound, max=bound).astype(held_as)


def setup_inputs(seed: int = 0) -> dict:
    key_list = jax.random.split(jax.random.key(seed), 8)
    tokens = noise(key_list[0], (TOKENS, D), 1.0, 6.0, ((0, 128),))
    out_grad = noise(key_list[1], (TOKENS, D), 1.0, 6.0, ((0, 128),))
    expert_ids = draw_expert_ids(jax.random.fold_in(key_list[7], 71), 0)
    probs = jnp.clip(0.049804688 + 0.3486328 * jax.random.uniform(key_list[3], (TOKENS, TOP), jnp.float32) ** steps_of(key_list[3], (TOKENS, TOP), ((0, 128),), -0.2, 0.2), 0.049804688, 0.3984375).astype(jnp.bfloat16)
    w_gate = noise(key_list[4], (EXPERTS, D, F), D ** -0.5, 0.09375, ((0, 128),))
    w_up = noise(key_list[5], (EXPERTS, D, F), D ** -0.5, 0.09375, ((0, 128),))
    w_down = noise(key_list[6], (EXPERTS, F, D), F ** -0.5, 0.1875, ((0, 128),))
    return {"tokens": tokens, "out_grad": out_grad, "expert_ids": expert_ids, "probs": probs, "w_gate": w_gate, "w_up": w_up, "w_down": w_down}


def expert_backward(rows_in, rows_grad, rows_prob, w_gate, w_up, w_down):
    gate = jnp.dot(rows_in, w_gate, preferred_element_type=jnp.float32)
    upward = jnp.dot(rows_in, w_up, preferred_element_type=jnp.float32)
    contract = (((1,), (1,)), ((), ()))
    d_hidden = lax.dot_general(rows_grad, w_down, contract, preferred_element_type=jnp.float32)
    sigmoid = jax.nn.sigmoid(gate)
    d_gate = (d_hidden * upward * (sigmoid * (1.0 + gate * (1.0 - sigmoid)))).astype(jnp.bfloat16)
    d_up = (d_hidden * (gate * sigmoid)).astype(jnp.bfloat16)
    back = lax.dot_general(d_gate, w_gate, contract, preferred_element_type=jnp.float32)
    back = back + lax.dot_general(d_up, w_up, contract, preferred_element_type=jnp.float32)
    return (rows_prob.astype(jnp.float32)[:, None] * back).astype(jnp.bfloat16)


def reference(tokens, out_grad, expert_ids, probs, w_gate, w_up, w_down):
    flat_ids = expert_ids.reshape(-1)
    flat_probs = probs.reshape(-1)
    most_rows = (TOKENS // TOK_DEV) * CAP
    positions = jnp.arange(most_rows, dtype=jnp.int32)

    def one_expert(total, expert):
        hits = flat_ids == expert
        count = jnp.sum(hits.astype(jnp.int32))
        routes = jnp.nonzero(hits, size=most_rows, fill_value=0)[0].astype(jnp.int32)
        valid = positions < count
        rows = (routes // TOP).astype(jnp.int32)
        rows_prob = jnp.where(valid, flat_probs[routes], jnp.zeros((), jnp.bfloat16))
        result = expert_backward(tokens[rows], out_grad[rows], rows_prob,
                                 w_gate[expert], w_up[expert], w_down[expert])
        addend = jnp.where(valid[:, None], result.astype(jnp.float32), jnp.zeros((), jnp.float32))
        return total.at[rows].add(addend), None

    start = jnp.zeros((TOKENS, D), jnp.float32)
    total, _ = lax.scan(one_expert, start, jnp.arange(EXPERTS, dtype=jnp.int32))
    return total.astype(jnp.bfloat16)
```

```python
import jax
import jax.numpy as jnp
from jax import lax
from jax.experimental import pallas as pl
from jax.experimental.pallas import tpu as pltpu
from jax.sharding import PartitionSpec as P

MESH = pl.DeviceIdType.MESH
D = 3584
F = 1024
TOK = 16
TILE = 128
THERE = ((4, 4, 4), (4, 3, 3), (2, 2, 2))
BACK = ((2, 2, 2), (4, 3, 3), (4, 4, 4))
NT = (((1,), (1,)), ((), ()))


def plan(waves):
    chunks, start = [], 0
    for wave in waves:
        row = []
        for kind, tiles in enumerate(wave):
            row.append((len(chunks) * 3 + kind, kind, start * TILE, tiles * TILE))
            start += tiles
        chunks.append(row)
    return chunks


def body(tokens, grads, ids, probs, w_gate, w_up, w_down, out, *scratch):
    there, back = plan(THERE), plan(BACK)
    n_there, n_back = 3 * len(THERE), 3 * len(BACK)
    scratch = list(scratch)

    def take(count):
        taken = scratch[:count]
        del scratch[:count]
        return taken

    x_buf, s_buf, g_buf = take(n_there), take(n_there), take(n_there)
    b_buf, r_buf, u_buf, ub_buf, v_buf, va_buf = (take(n_back) for _ in range(6))
    m_buf = take(3)
    p_buf, q_buf = take(3), take(3)
    to_first, from_first = take(2), take(2)
    tok_v, grad_v, ids_v, prob_v, wg_v, wu_v, wd_v = take(7)
    gate_acc, up_acc, hid_acc = take(3)
    dg_v, du_v = take(3), take(3)
    in_sem, send_sem, m_sem, xa_sem, xb_sem, xc_sem, rc_sem, rb_sem, ra_sem = take(9)

    group, local = lax.axis_index("group"), lax.axis_index("local")
    here = (group // 2, local // 4, local % 4)
    core = group % 2

    def device(axis, step, other):
        x, y, z = (lax.rem(c + (step if a == axis else 0), 4) for a, c in enumerate(here))
        k = lax.rem(core + other, 2)
        return (x * 2 + k, y * 4 + z)

    partners = [(axis, step, other) for axis in range(3) for step in (1, 2, 3) for other in (0, 1)]
    partners.append((0, 0, 1))
    barrier = pltpu.get_barrier_semaphore()
    for partner in partners:
        pl.semaphore_signal(barrier, inc=1, device_id=device(*partner), device_id_type=MESH)

    loads = [
        pltpu.make_async_copy(src, dst, in_sem.at[i])
        for i, (src, dst) in enumerate(
            (
                (ids, ids_v),
                (probs, prob_v),
                (tokens, tok_v),
                (grads, grad_v),
                (w_gate.at[0], wg_v),
                (w_up.at[0], wu_v),
                (w_down.at[0], wd_v),
            )
        )
    ]
    for load in loads:
        load.start()

    def send(src, dst, sem, recv, target):
        pltpu.make_async_remote_copy(
            src_ref=src,
            dst_ref=dst,
            send_sem=sem,
            recv_sem=recv,
            device_id=device(*target),
            device_id_type=MESH,
        ).start()

    def await_bytes(ref, sem):
        pltpu.make_async_copy(ref, ref, sem).wait()

    loads[0].wait()
    loads[1].wait()
    lane = lax.broadcasted_iota(jnp.int32, (TOK, 128), 1)
    dense = jnp.zeros((TOK, 128), jnp.float32)
    weight = prob_v[...].astype(jnp.float32)
    named = ids_v[...]
    for k in range(8):
        dense += jnp.where(named[:, k : k + 1] == lane, weight[:, k : k + 1], 0.0)
    earlier = lax.broadcasted_iota(jnp.int32, (TOK, TOK), 0) > lax.broadcasted_iota(jnp.int32, (TOK, TOK), 1)
    rank = jnp.dot(
        earlier.astype(jnp.bfloat16),
        (dense > 0.0).astype(jnp.bfloat16),
        preferred_element_type=jnp.float32,
    )
    meta = jnp.where(rank > 0.5, -dense, dense).astype(jnp.bfloat16)
    for kind in range(3):
        m_buf[kind][0:TOK] = meta
    def as_kind(row, kind):
        z, y, x = (jnp.bitwise_and(lax.shift_right_logical(row, shift), 3) for shift in (6, 3, 1))
        step = (x, y, z)
        moved = step[(kind + 2) % 3] * 64 + step[(kind + 1) % 3] * 8 + step[kind] * 2
        return moved + jnp.bitwise_and(row, 33)

    down = lax.broadcasted_iota(jnp.int32, (256, 256), 0)
    across = lax.broadcasted_iota(jnp.int32, (256, 256), 1)
    for kind in (1, 2):
        to_first[kind - 1][...] = (as_kind(down, kind) == across).astype(jnp.bfloat16)
        from_first[kind - 1][...] = (as_kind(across, kind) == down).astype(jnp.bfloat16)
    loads[2].wait()
    loads[3].wait()
    for row in there:
        for n, kind, start, width in row:
            x_buf[n][0, 0:TOK] = tok_v[:, start : start + width]
            x_buf[n][1, 0:TOK] = grad_v[:, start : start + width]

    pl.semaphore_wait(barrier, len(partners))

    for w, row in enumerate(there):
        for n, kind, start, width in row:
            for step in (2, 1, 3):
                rows = pl.ds(step * TOK, TOK)
                if w == 0:
                    send(
                        m_buf[kind].at[0:TOK], m_buf[kind].at[rows], send_sem.at[0], m_sem.at[kind], (kind, step, 0)
                    )
                send(
                    x_buf[n].at[:, 0:TOK], x_buf[n].at[:, rows], send_sem.at[1], xa_sem.at[n], (kind, step, 0)
                )

    for w, row in enumerate(there):
        for n, kind, start, width in row:
            second = (kind + 1) % 3
            if w == 0:
                await_bytes(m_buf[kind].at[TOK : 4 * TOK], m_sem.at[kind])
            await_bytes(x_buf[n].at[:, TOK : 4 * TOK], xa_sem.at[n])
            for step in (2, 1, 3):
                rows = pl.ds(step * 4 * TOK, 4 * TOK)
                if w == 0:
                    send(
                        m_buf[kind].at[0 : 4 * TOK],
                        m_buf[kind].at[rows],
                        send_sem.at[2],
                        m_sem.at[3 + kind],
                        (second, step, 0),
                    )
                send(
                    x_buf[n].at[:, 0 : 4 * TOK],
                    x_buf[n].at[:, rows],
                    send_sem.at[3],
                    xb_sem.at[n],
                    (second, step, 0),
                )

    def make_tables(kind):
        third = (kind + 2) % 3
        await_bytes(m_buf[kind].at[4 * TOK : 16 * TOK], m_sem.at[3 + kind])
        gathered = m_buf[kind][...]

        def expert(slot):
            block = lax.shift_right_logical(slot, 5)
            step = lax.shift_right_logical(block, 1)
            k = jnp.bitwise_and(core + jnp.bitwise_and(block, 1), 1)
            x, y, z = (jnp.bitwise_and(c + step, 3) if a == third else c for a, c in enumerate(here))
            return (x * 2 + k) * 16 + y * 4 + z

        def table(slot, token, found):
            source = jnp.bitwise_and(lax.shift_right_logical(slot, 1), 15)
            same = source == lax.shift_right_logical(token, 4)
            signed = jnp.where(jnp.bitwise_and(slot, 1) == 1, -found, found)
            return jnp.where(same & (signed > 0.0), signed, 0.0)

        def iota(shape, axis):
            return lax.broadcasted_iota(jnp.int32, shape, axis)

        picks = (iota((128, 256), 0) == expert(iota((128, 256), 1))).astype(jnp.bfloat16)
        found = jnp.dot(gathered, picks, preferred_element_type=jnp.float32)
        q_buf[kind][...] = table(iota((256, 256), 1), iota((256, 256), 0), found).astype(jnp.bfloat16)
        picks = (iota((256, 128), 1) == expert(iota((256, 128), 0))).astype(jnp.bfloat16)
        found = lax.dot_general(picks, gathered, NT, preferred_element_type=jnp.float32)
        taken = table(iota((256, 256), 0), iota((256, 256), 1), found)
        p_buf[kind][...] = (taken > 0.0).astype(jnp.bfloat16)

    def block(step, other):
        return pl.ds((step * 2 + other) * 32, 32)

    exchange = [(2, 0), (2, 1), (1, 0), (3, 0), (1, 1), (3, 1), (0, 1)]

    def pack(n, kind):
        third = (kind + 2) % 3
        await_bytes(x_buf[n].at[:, 4 * TOK : 16 * TOK], xb_sem.at[n])
        for half in range(2):
            rows = jnp.dot(p_buf[kind][...], x_buf[n][half], preferred_element_type=jnp.float32).astype(jnp.bfloat16)
            g_buf[n][half, 0:32] = rows[0:32]
            s_buf[n][half] = rows
        for step, other in exchange:
            send(
                s_buf[n].at[:, block(step, other)],
                g_buf[n].at[:, block(step, other)],
                send_sem.at[4],
                xc_sem.at[n],
                (third, step, other),
            )

    def absorb(n, kind, start, width, first):
        await_bytes(g_buf[n].at[:, 32:256], xc_sem.at[n])
        if kind:
            for half in range(2):
                g_buf[n][half] = jnp.dot(
                    to_first[kind - 1][...], g_buf[n][half], preferred_element_type=jnp.float32
                ).astype(jnp.bfloat16)

        def columns(i, carry):
            cols = pl.ds(pl.multiple_of(i * 256, 256), 256)
            rows_in, rows_grad = g_buf[n][0], g_buf[n][1]
            gate = jnp.dot(rows_in, wg_v[start : start + width, cols], preferred_element_type=jnp.float32)
            upward = jnp.dot(rows_in, wu_v[start : start + width, cols], preferred_element_type=jnp.float32)
            hidden = lax.dot_general(
                rows_grad, wd_v[cols, start : start + width], NT, preferred_element_type=jnp.float32
            )
            if first:
                gate_acc[:, cols] = gate
                up_acc[:, cols] = upward
                hid_acc[:, cols] = hidden
            else:
                gate_acc[:, cols] += gate
                up_acc[:, cols] += upward
                hid_acc[:, cols] += hidden
            return carry

        lax.fori_loop(0, F // 256, columns, 0)

    def absorb_wave(w):
        if w == 0:
            for load in loads[4:]:
                load.wait()
        for n, kind, start, width in there[w]:
            absorb(n, kind, start, width, n == 0)

    for w, row in enumerate(there):
        for n, kind, start, width in row:
            if w == 0:
                make_tables(kind)
            pack(n, kind)
        if w >= 1:
            absorb_wave(w - 1)
    absorb_wave(len(there) - 1)

    def middle(i, carry):
        cols = pl.ds(pl.multiple_of(i * 256, 256), 256)
        gate, upward, hidden = gate_acc[:, cols], up_acc[:, cols], hid_acc[:, cols]
        s = jax.nn.sigmoid(gate)
        d_gate = (hidden * upward * (s * (1.0 + gate * (1.0 - s)))).astype(jnp.bfloat16)
        d_up = (hidden * (gate * s)).astype(jnp.bfloat16)
        dg_v[0][:, cols] = d_gate
        du_v[0][:, cols] = d_up
        for kind in (1, 2):
            order = from_first[kind - 1][...]
            dg_v[kind][:, cols] = jnp.dot(order, d_gate, preferred_element_type=jnp.float32).astype(jnp.bfloat16)
            du_v[kind][:, cols] = jnp.dot(order, d_up, preferred_element_type=jnp.float32).astype(jnp.bfloat16)
        return carry

    lax.fori_loop(0, F // 256, middle, 0)

    def give(n, kind, start, width):
        third = (kind + 2) % 3
        result = lax.dot_general(dg_v[kind][...], wg_v[start : start + width], NT, preferred_element_type=jnp.float32)
        result += lax.dot_general(du_v[kind][...], wu_v[start : start + width], NT, preferred_element_type=jnp.float32)
        result = result.astype(jnp.bfloat16)
        r_buf[n][0:32] = result[0:32]
        b_buf[n][...] = result
        for step, other in exchange:
            send(
                b_buf[n].at[block(step, other)],
                r_buf[n].at[block(step, other)],
                send_sem.at[5],
                rc_sem.at[n],
                (third, (4 - step) % 4, other),
            )

    def combine(n, kind):
        second = (kind + 1) % 3
        await_bytes(r_buf[n].at[32:256], rc_sem.at[n])
        part = jnp.dot(q_buf[kind][...], r_buf[n][...], preferred_element_type=jnp.float32)
        u_buf[n][...] = part.astype(jnp.bfloat16)
        for step in (2, 1, 3):
            send(
                u_buf[n].at[pl.ds(step * 64, 64)],
                ub_buf[n].at[pl.ds(step * 64, 64)],
                send_sem.at[6],
                rb_sem.at[n],
                (second, 4 - step, 0),
            )

    def reduce_second(n, kind):
        await_bytes(ub_buf[n].at[64:256], rb_sem.at[n])
        part = u_buf[n][0:64].astype(jnp.float32)
        for step in (1, 2, 3):
            part += ub_buf[n][step * 64 : step * 64 + 64].astype(jnp.float32)
        v_buf[n][...] = part.astype(jnp.bfloat16)
        for step in (2, 1, 3):
            send(
                v_buf[n].at[pl.ds(step * TOK, TOK)],
                va_buf[n].at[pl.ds(step * TOK, TOK)],
                send_sem.at[7],
                ra_sem.at[n],
                (kind, 4 - step, 0),
            )

    def finish(n, start, width):
        await_bytes(va_buf[n].at[TOK : 4 * TOK], ra_sem.at[n])
        part = v_buf[n][0:TOK].astype(jnp.float32)
        for step in (1, 2, 3):
            part += va_buf[n][step * TOK : step * TOK + TOK].astype(jnp.float32)
        out[:, start : start + width] = part.astype(jnp.bfloat16)

    waves = len(back)
    for w in range(waves):
        for n, kind, start, width in back[w]:
            give(n, kind, start, width)
    for w in range(waves + 2):
        if w < waves:
            for n, kind, start, width in back[w]:
                combine(n, kind)
        if 1 <= w <= waves:
            for n, kind, start, width in back[w - 1]:
                reduce_second(n, kind)
        if w >= 2:
            for n, kind, start, width in back[w - 2]:
                finish(n, start, width)

    for row in there:
        for n, kind, start, width in row:
            if n < 3:
                await_bytes(m_buf[kind].at[0 : 3 * TOK], send_sem.at[0])
                await_bytes(m_buf[kind].at[0 : 12 * TOK], send_sem.at[2])
            await_bytes(x_buf[n].at[:, 0 : 3 * TOK], send_sem.at[1])
            await_bytes(x_buf[n].at[:, 0 : 12 * TOK], send_sem.at[3])
            await_bytes(s_buf[n].at[:, 32:256], send_sem.at[4])
    for row in back:
        for n, kind, start, width in row:
            await_bytes(b_buf[n].at[32:256], send_sem.at[5])
            await_bytes(u_buf[n].at[64:256], send_sem.at[6])
            await_bytes(v_buf[n].at[TOK : 4 * TOK], send_sem.at[7])


def local_part(tokens, out_grad, expert_ids, probs, w_gate, w_up, w_down):
    there = [c[3] for row in plan(THERE) for c in row]
    back = [c[3] for row in plan(BACK) for c in row]
    bf16, f32 = jnp.bfloat16, jnp.float32
    scratch = (
        [pltpu.VMEM((2, 256, w), bf16) for _ in range(3) for w in there]
        + [pltpu.VMEM((256, w), bf16) for _ in range(4) for w in back]
        + [pltpu.VMEM((64, w), bf16) for _ in range(2) for w in back]
        + [pltpu.VMEM((256, 128), bf16)] * 3
        + [pltpu.VMEM((256, 256), bf16)] * 10
        + [
            pltpu.VMEM((TOK, D), bf16),
            pltpu.VMEM((TOK, D), bf16),
            pltpu.VMEM((TOK, 8), jnp.int32),
            pltpu.VMEM((TOK, 8), bf16),
            pltpu.VMEM((D, F), bf16),
            pltpu.VMEM((D, F), bf16),
            pltpu.VMEM((F, D), bf16),
        ]
        + [pltpu.VMEM((256, F), f32)] * 3
        + [pltpu.VMEM((256, F), bf16)] * 6
        + [
            pltpu.SemaphoreType.DMA((7,)),
            pltpu.SemaphoreType.DMA((8,)),
            pltpu.SemaphoreType.DMA((6,)),
            pltpu.SemaphoreType.DMA((len(there),)),
            pltpu.SemaphoreType.DMA((len(there),)),
            pltpu.SemaphoreType.DMA((len(there),)),
            pltpu.SemaphoreType.DMA((len(back),)),
            pltpu.SemaphoreType.DMA((len(back),)),
            pltpu.SemaphoreType.DMA((len(back),)),
        ]
    )
    return pl.pallas_call(
        body,
        out_shape=jax.ShapeDtypeStruct((TOK, D), bf16),
        in_specs=[pl.BlockSpec(memory_space=pl.ANY)] * 7,
        out_specs=pl.BlockSpec(memory_space=pltpu.VMEM),
        scratch_shapes=scratch,
        compiler_params=pltpu.CompilerParams(
            collective_id=0, has_side_effects=True, vmem_limit_bytes=60 * 1024 * 1024
        ),
        cost_estimate=pl.CostEstimate(flops=2 * 256 * D * F * 5, bytes_accessed=3 * D * F * 2, transcendentals=256 * F),
    )(tokens, out_grad, expert_ids, probs, w_gate, w_up, w_down)


def solution(mesh):
    flat = P(("group", "local"), None)
    deep = P(("group", "local"), None, None)
    return jax.shard_map(
        local_part,
        mesh=mesh,
        in_specs=(flat, flat, flat, flat, deep, deep, deep),
        out_specs=flat,
        check_vma=False,
    )
```

```python
import jax
import jax.numpy as jnp
from jax import lax
from jax.experimental import pallas as pl
from jax.experimental.pallas import tpu as pltpu
from jax.sharding import PartitionSpec as P

MESH = pl.DeviceIdType.MESH
D = 3584
F = 1024
TOK = 16
TILE = 128
THERE = ((4, 4, 4), (4, 3, 3), (2, 2, 2))
BACK = ((4, 4, 4), (4, 3, 3), (2, 2, 2))
N_STEP = 512
LAST_STEP = 256
NT = (((1,), (1,)), ((), ()))


def plan(waves):
    chunks, start = [], 0
    for wave in waves:
        row = []
        for kind, tiles in enumerate(wave):
            row.append((len(chunks) * 3 + kind, kind, start * TILE, tiles * TILE))
            start += tiles
        chunks.append(row)
    return chunks


def body(tokens, grads, ids, probs, w_gate, w_up, w_down, out, *scratch):
    there, back = plan(THERE), plan(BACK)
    n_there, n_back = 3 * len(THERE), 3 * len(BACK)
    scratch = list(scratch)

    def take(count):
        taken = scratch[:count]
        del scratch[:count]
        return taken

    x_buf, s_buf, g_buf = take(n_there), take(n_there), take(len(THERE))
    b_buf, r_buf, u_buf, ub_buf, v_buf, va_buf = (take(n_back) for _ in range(6))
    m_buf = take(3)
    p_buf, q_buf = take(3), take(3)
    to_first, from_first = take(2), take(2)
    ids_v, prob_v, wg_v, wu_v, wd_v = take(5)
    gate_acc, up_acc, hid_acc = take(3)
    dg_v, du_v = take(3), take(3)
    in_sem, x_sem, send_sem, m_sem, xa_sem, xb_sem, xc_sem, rc_sem, rb_sem, ra_sem = take(10)

    group, local = lax.axis_index("group"), lax.axis_index("local")
    here = (group // 2, local // 4, local % 4)
    core = group % 2

    def device(axis, step, other):
        x, y, z = (lax.rem(c + (step if a == axis else 0), 4) for a, c in enumerate(here))
        k = lax.rem(core + other, 2)
        return (x * 2 + k, y * 4 + z)

    partners = [(axis, step, other) for axis in range(3) for step in (1, 2, 3) for other in (0, 1)]
    partners.append((0, 0, 1))
    barrier = pltpu.get_barrier_semaphore()
    for partner in partners:
        pl.semaphore_signal(barrier, inc=1, device_id=device(*partner), device_id_type=MESH)

    loads = []

    def load(src, dst, sem):
        loads.append(pltpu.make_async_copy(src, dst, sem))
        loads[-1].start()

    for row in there:
        for n, kind, start, width in row:
            cols = slice(start, start + width)
            load(tokens.at[:, cols], x_buf[n].at[0, 0:TOK], x_sem.at[0, n])
            load(grads.at[:, cols], x_buf[n].at[1, 0:TOK], x_sem.at[1, n])
    load(ids, ids_v, in_sem.at[0])
    load(probs, prob_v, in_sem.at[1])

    def send(src, dst, sem, recv, target):
        pltpu.make_async_remote_copy(
            src_ref=src,
            dst_ref=dst,
            send_sem=sem,
            recv_sem=recv,
            device_id=device(*target),
            device_id_type=MESH,
        ).start()

    def await_bytes(ref, sem):
        pltpu.make_async_copy(ref, ref, sem).wait()

    for copy in loads[: 2 * n_there]:
        copy.wait()
    pl.semaphore_wait(barrier, len(partners))

    for row in there:
        for n, kind, start, width in row:
            for step in (2, 1, 3):
                send(
                    x_buf[n].at[:, 0:TOK],
                    x_buf[n].at[:, pl.ds(step * TOK, TOK)],
                    send_sem.at[1],
                    xa_sem.at[n],
                    (kind, step, 0),
                )

    for copy in loads[2 * n_there : 2 * n_there + 2]:
        copy.wait()
    lane = lax.broadcasted_iota(jnp.int32, (TOK, 128), 1)
    dense = jnp.zeros((TOK, 128), jnp.float32)
    same = (
        lax.broadcasted_iota(jnp.int32, (TOK, TOK), 0) == lax.broadcasted_iota(jnp.int32, (TOK, TOK), 1)
    ).astype(jnp.bfloat16)
    weight = lax.dot_general(same, prob_v[...], NT, preferred_element_type=jnp.float32)
    named = lax.dot_general(
        same, ids_v[...].astype(jnp.bfloat16), NT, preferred_element_type=jnp.float32
    ).astype(jnp.int32)
    for k in range(8):
        dense += jnp.where(named[:, k : k + 1] == lane, weight[:, k : k + 1], 0.0)
    earlier = lax.broadcasted_iota(jnp.int32, (TOK, TOK), 0) > lax.broadcasted_iota(jnp.int32, (TOK, TOK), 1)
    rank = jnp.dot(
        earlier.astype(jnp.bfloat16),
        (dense > 0.0).astype(jnp.bfloat16),
        preferred_element_type=jnp.float32,
    )
    meta = jnp.where(rank > 0.5, -dense, dense).astype(jnp.bfloat16)
    for kind in range(3):
        m_buf[kind][0:TOK] = meta
    for kind in range(3):
        for step in (2, 1, 3):
            rows = pl.ds(step * TOK, TOK)
            send(m_buf[kind].at[0:TOK], m_buf[kind].at[rows], send_sem.at[0], m_sem.at[kind], (kind, step, 0))
    for src, dst, sem in ((w_gate, wg_v, 2), (w_up, wu_v, 3), (w_down, wd_v, 4)):
        load(src.at[0], dst, in_sem.at[sem])

    def as_kind(row, kind):
        z, y, x = (jnp.bitwise_and(lax.shift_right_logical(row, shift), 3) for shift in (6, 3, 1))
        step = (x, y, z)
        moved = step[(kind + 2) % 3] * 64 + step[(kind + 1) % 3] * 8 + step[kind] * 2
        return moved + jnp.bitwise_and(row, 33)

    down = lax.broadcasted_iota(jnp.int32, (256, 256), 0)
    across = lax.broadcasted_iota(jnp.int32, (256, 256), 1)
    for kind in (1, 2):
        to_first[kind - 1][...] = (as_kind(down, kind) == across).astype(jnp.bfloat16)
        from_first[kind - 1][...] = (as_kind(across, kind) == down).astype(jnp.bfloat16)
    for w, row in enumerate(there):
        for n, kind, start, width in row:
            second = (kind + 1) % 3
            if w == 0:
                await_bytes(m_buf[kind].at[TOK : 4 * TOK], m_sem.at[kind])
            await_bytes(x_buf[n].at[:, TOK : 4 * TOK], xa_sem.at[n])
            for step in (2, 1, 3):
                rows = pl.ds(step * 4 * TOK, 4 * TOK)
                if w == 0:
                    send(
                        m_buf[kind].at[0 : 4 * TOK],
                        m_buf[kind].at[rows],
                        send_sem.at[2],
                        m_sem.at[3 + kind],
                        (second, step, 0),
                    )
                send(
                    x_buf[n].at[:, 0 : 4 * TOK], x_buf[n].at[:, rows], send_sem.at[3], xb_sem.at[n], (second, step, 0)
                )

    def make_tables(kind):
        third = (kind + 2) % 3
        await_bytes(m_buf[kind].at[4 * TOK : 16 * TOK], m_sem.at[3 + kind])
        gathered = m_buf[kind][...]

        def expert(slot):
            block = lax.shift_right_logical(slot, 5)
            step = lax.shift_right_logical(block, 1)
            k = jnp.bitwise_and(core + jnp.bitwise_and(block, 1), 1)
            x, y, z = (jnp.bitwise_and(c + step, 3) if a == third else c for a, c in enumerate(here))
            return (x * 2 + k) * 16 + y * 4 + z

        def table(slot, token, found):
            source = jnp.bitwise_and(lax.shift_right_logical(slot, 1), 15)
            same = source == lax.shift_right_logical(token, 4)
            signed = jnp.where(jnp.bitwise_and(slot, 1) == 1, -found, found)
            return jnp.where(same & (signed > 0.0), signed, 0.0)

        def iota(shape, axis):
            return lax.broadcasted_iota(jnp.int32, shape, axis)

        picks = (iota((128, 256), 0) == expert(iota((128, 256), 1))).astype(jnp.bfloat16)
        found = jnp.dot(gathered, picks, preferred_element_type=jnp.float32)
        q_buf[kind][...] = table(iota((256, 256), 1), iota((256, 256), 0), found).astype(jnp.bfloat16)
        picks = (iota((256, 128), 1) == expert(iota((256, 128), 0))).astype(jnp.bfloat16)
        found = lax.dot_general(picks, gathered, NT, preferred_element_type=jnp.float32)
        taken = table(iota((256, 256), 0), iota((256, 256), 1), found)
        p_buf[kind][...] = (taken > 0.0).astype(jnp.bfloat16)

    def block(step, other):
        return pl.ds((step * 2 + other) * 32, 32)

    exchange = [(2, 0), (2, 1), (1, 0), (3, 0), (1, 1), (3, 1), (0, 1)]

    def landing(w, n, start, width):
        at = start - there[w][0][2]
        return g_buf[w].at[:, :, at : at + width]

    def pack(w, n, kind, start, width):
        third = (kind + 2) % 3
        await_bytes(x_buf[n].at[:, 4 * TOK : 16 * TOK], xb_sem.at[n])
        land = landing(w, n, start, width)
        for half in range(2):
            rows = jnp.dot(p_buf[kind][...], x_buf[n][half], preferred_element_type=jnp.float32).astype(jnp.bfloat16)
            land[half, 0:32] = rows[0:32]
            s_buf[n][half] = rows
        for step, other in exchange:
            send(
                s_buf[n].at[:, block(step, other)],
                land.at[:, block(step, other)],
                send_sem.at[4],
                xc_sem.at[n],
                (third, step, other),
            )

    def absorb(w):
        if w == 0:
            for copy in loads[2 * n_there + 2 :]:
                copy.wait()
        for n, kind, start, width in there[w]:
            land = landing(w, n, start, width)
            await_bytes(land.at[:, 32:256], xc_sem.at[n])
            if kind:
                for half in range(2):
                    land[half] = jnp.dot(
                        to_first[kind - 1][...], land[half], preferred_element_type=jnp.float32
                    ).astype(jnp.bfloat16)
        first, span = there[w][0][2], sum(THERE[w]) * TILE

        def columns(cols):
            rows_in, rows_grad = g_buf[w][0], g_buf[w][1]
            gate = jnp.dot(rows_in, wg_v[first : first + span, cols], preferred_element_type=jnp.float32)
            upward = jnp.dot(rows_in, wu_v[first : first + span, cols], preferred_element_type=jnp.float32)
            hidden = lax.dot_general(
                rows_grad, wd_v[cols, first : first + span], NT, preferred_element_type=jnp.float32
            )
            if w > 0:
                gate += gate_acc[:, cols]
                upward += up_acc[:, cols]
                hidden += hid_acc[:, cols]
            return gate, upward, hidden

        def store(i, carry):
            cols = pl.ds(pl.multiple_of(i * N_STEP, N_STEP), N_STEP)
            gate_acc[:, cols], up_acc[:, cols], hid_acc[:, cols] = columns(cols)
            return carry

        if w < len(there) - 1:
            lax.fori_loop(0, F // N_STEP, store, 0)
            return
        for at in range(0, F, LAST_STEP):
            cols = slice(at, at + LAST_STEP)
            gate, upward, hidden = columns(cols)
            s = jax.nn.sigmoid(gate)
            dg_v[0][:, cols] = (hidden * upward * (s * (1.0 + gate * (1.0 - s)))).astype(jnp.bfloat16)
            du_v[0][:, cols] = (hidden * (gate * s)).astype(jnp.bfloat16)

    for w, row in enumerate(there):
        for n, kind, start, width in row:
            if w == 0:
                make_tables(kind)
            pack(w, n, kind, start, width)
        if w >= 1:
            absorb(w - 1)
    absorb(len(there) - 1)

    def reorder(kind):
        order = from_first[kind - 1][...]
        for held in (dg_v, du_v):
            held[kind][...] = jnp.dot(order, held[0][...], preferred_element_type=jnp.float32).astype(jnp.bfloat16)

    def give(n, kind, start, width):
        third = (kind + 2) % 3
        if 0 < n < 3:
            reorder(kind)
        result = lax.dot_general(dg_v[kind][...], wg_v[start : start + width], NT, preferred_element_type=jnp.float32)
        result += lax.dot_general(du_v[kind][...], wu_v[start : start + width], NT, preferred_element_type=jnp.float32)
        result = result.astype(jnp.bfloat16)
        r_buf[n][0:32] = result[0:32]
        b_buf[n][...] = result
        for step, other in exchange:
            send(
                b_buf[n].at[block(step, other)],
                r_buf[n].at[block(step, other)],
                send_sem.at[5],
                rc_sem.at[n],
                (third, (4 - step) % 4, other),
            )

    def combine(n, kind):
        second = (kind + 1) % 3
        await_bytes(r_buf[n].at[32:256], rc_sem.at[n])
        part = jnp.dot(q_buf[kind][...], r_buf[n][...], preferred_element_type=jnp.float32)
        u_buf[n][...] = part.astype(jnp.bfloat16)
        for step in (2, 1, 3):
            rows = pl.ds(step * 64, 64)
            send(u_buf[n].at[rows], ub_buf[n].at[rows], send_sem.at[6], rb_sem.at[n], (second, 4 - step, 0))

    def reduce_second(n, kind):
        await_bytes(ub_buf[n].at[64:256], rb_sem.at[n])
        part = u_buf[n][0:64].astype(jnp.float32)
        for step in (1, 2, 3):
            part += ub_buf[n][step * 64 : step * 64 + 64].astype(jnp.float32)
        v_buf[n][...] = part.astype(jnp.bfloat16)
        for step in (2, 1, 3):
            send(
                v_buf[n].at[pl.ds(step * TOK, TOK)],
                va_buf[n].at[pl.ds(step * TOK, TOK)],
                send_sem.at[7],
                ra_sem.at[n],
                (kind, 4 - step, 0),
            )

    def finish(n, start, width):
        await_bytes(va_buf[n].at[TOK : 4 * TOK], ra_sem.at[n])
        part = v_buf[n][0:TOK].astype(jnp.float32)
        for step in (1, 2, 3):
            part += va_buf[n][step * TOK : step * TOK + TOK].astype(jnp.float32)
        out[:, start : start + width] = part

    waves = len(back)
    for w in range(waves + 3):
        if w < waves:
            for n, kind, start, width in back[w]:
                give(n, kind, start, width)
        if 1 <= w <= waves:
            for n, kind, start, width in back[w - 1]:
                combine(n, kind)
        if 2 <= w <= waves + 1:
            for n, kind, start, width in back[w - 2]:
                reduce_second(n, kind)
        if w >= 3:
            for n, kind, start, width in back[w - 3]:
                finish(n, start, width)

    for row in there:
        for n, kind, start, width in row:
            if n < 3:
                await_bytes(m_buf[kind].at[0 : 3 * TOK], send_sem.at[0])
                await_bytes(m_buf[kind].at[0 : 12 * TOK], send_sem.at[2])
            await_bytes(x_buf[n].at[:, 0 : 3 * TOK], send_sem.at[1])
            await_bytes(x_buf[n].at[:, 0 : 12 * TOK], send_sem.at[3])
            await_bytes(s_buf[n].at[:, 32:256], send_sem.at[4])
    for row in back:
        for n, kind, start, width in row:
            await_bytes(b_buf[n].at[32:256], send_sem.at[5])
            await_bytes(u_buf[n].at[64:256], send_sem.at[6])
            await_bytes(v_buf[n].at[TOK : 4 * TOK], send_sem.at[7])


def local_part(tokens, out_grad, expert_ids, probs, w_gate, w_up, w_down):
    there = [c[3] for row in plan(THERE) for c in row]
    back = [c[3] for row in plan(BACK) for c in row]
    bf16, f32 = jnp.bfloat16, jnp.float32
    scratch = (
        [pltpu.VMEM((2, 256, w), bf16) for _ in range(2) for w in there]
        + [pltpu.VMEM((2, 256, sum(wave) * TILE), bf16) for wave in THERE]
        + [pltpu.VMEM((256, w), bf16) for _ in range(4) for w in back]
        + [pltpu.VMEM((64, w), bf16) for _ in range(2) for w in back]
        + [pltpu.VMEM((256, 128), bf16)] * 3
        + [pltpu.VMEM((256, 256), bf16)] * 10
        + [
            pltpu.VMEM((8, TOK), jnp.int32),
            pltpu.VMEM((8, TOK), bf16),
            pltpu.VMEM((D, F), bf16),
            pltpu.VMEM((D, F), bf16),
            pltpu.VMEM((F, D), bf16),
        ]
        + [pltpu.VMEM((256, F), f32)] * 3
        + [pltpu.VMEM((256, F), bf16)] * 6
        + [
            pltpu.SemaphoreType.DMA((5,)),
            pltpu.SemaphoreType.DMA((2, len(there))),
            pltpu.SemaphoreType.DMA((8,)),
            pltpu.SemaphoreType.DMA((6,)),
            pltpu.SemaphoreType.DMA((len(there),)),
            pltpu.SemaphoreType.DMA((len(there),)),
            pltpu.SemaphoreType.DMA((len(there),)),
            pltpu.SemaphoreType.DMA((len(back),)),
            pltpu.SemaphoreType.DMA((len(back),)),
            pltpu.SemaphoreType.DMA((len(back),)),
        ]
    )
    total = pl.pallas_call(
        body,
        out_shape=jax.ShapeDtypeStruct((TOK, D), f32),
        in_specs=[pl.BlockSpec(memory_space=pl.ANY)] * 7,
        out_specs=pl.BlockSpec(memory_space=pltpu.VMEM),
        scratch_shapes=scratch,
        compiler_params=pltpu.CompilerParams(
            collective_id=0, has_side_effects=True, vmem_limit_bytes=60 * 1024 * 1024
        ),
        cost_estimate=pl.CostEstimate(flops=2 * 256 * D * F * 5, bytes_accessed=3 * D * F * 2, transcendentals=256 * F),
    )(tokens, out_grad, expert_ids.T, probs.T, w_gate, w_up, w_down)
    return total.astype(bf16)


def solution(mesh):
    flat = P(("group", "local"), None)
    deep = P(("group", "local"), None, None)
    return jax.shard_map(
        local_part,
        mesh=mesh,
        in_specs=(flat, flat, flat, flat, deep, deep, deep),
        out_specs=flat,
        check_vma=False,
    )
```

```python
import jax
import jax.numpy as jnp
from jax import lax
from jax.experimental import pallas as pl
from jax.experimental.pallas import tpu as pltpu
from jax.sharding import PartitionSpec as P

MESH = pl.DeviceIdType.MESH
D = 3584
F = 1024
TOK = 16
TILE = 128
THERE = ((2, 2, 2), (4, 4, 4), (4, 3, 3))
BACK = ((4, 4, 4), (4, 3, 3), (2, 2, 2))
N_STEP = 512
LAST_STEP = 256
NT = (((1,), (1,)), ((), ()))


def plan(waves):
    chunks, start = [], 0
    for wave in waves:
        row = []
        for kind, tiles in enumerate(wave):
            row.append((len(chunks) * 3 + kind, kind, start * TILE, tiles * TILE))
            start += tiles
        chunks.append(row)
    return chunks


def body(tokens, grads, ids, probs, w_gate, w_up, w_down, out, *scratch):
    there, back = plan(THERE), plan(BACK)
    n_there, n_back = 3 * len(THERE), 3 * len(BACK)
    scratch = list(scratch)

    def take(count):
        taken = scratch[:count]
        del scratch[:count]
        return taken

    x_buf, s_buf, g_buf = take(n_there), take(n_there), take(len(THERE))
    b_buf, r_buf, u_buf, ub_buf, v_buf, va_buf = (take(n_back) for _ in range(6))
    m_buf = take(3)
    p_buf, q_buf = take(3), take(3)
    to_first, from_first = take(2), take(2)
    ids_v, prob_v, wg_v, wu_v, wd_v = take(5)
    gate_acc, up_acc, hid_acc = take(3)
    dg_v, du_v = take(3), take(3)
    in_sem, x_sem, send_sem, m_sem, xa_sem, xb_sem, xc_sem, rc_sem, rb_sem, ra_sem = take(10)

    group, local = lax.axis_index("group"), lax.axis_index("local")
    here = (group // 2, local // 4, local % 4)
    core = group % 2

    def device(axis, step, other):
        x, y, z = (lax.rem(c + (step if a == axis else 0), 4) for a, c in enumerate(here))
        k = lax.rem(core + other, 2)
        return (x * 2 + k, y * 4 + z)

    partners = [(axis, step, other) for axis in range(3) for step in (1, 2, 3) for other in (0, 1)]
    partners.append((0, 0, 1))
    barrier = pltpu.get_barrier_semaphore()
    for partner in partners:
        pl.semaphore_signal(barrier, inc=1, device_id=device(*partner), device_id_type=MESH)

    loads = []

    def load(src, dst, sem):
        loads.append(pltpu.make_async_copy(src, dst, sem))
        loads[-1].start()

    for row in there:
        for n, kind, start, width in row:
            cols = slice(start, start + width)
            load(tokens.at[:, cols], x_buf[n].at[0, 0:TOK], x_sem.at[0, n])
            load(grads.at[:, cols], x_buf[n].at[1, 0:TOK], x_sem.at[1, n])
    load(ids, ids_v, in_sem.at[0])
    load(probs, prob_v, in_sem.at[1])

    def send(src, dst, sem, recv, target):
        pltpu.make_async_remote_copy(
            src_ref=src,
            dst_ref=dst,
            send_sem=sem,
            recv_sem=recv,
            device_id=device(*target),
            device_id_type=MESH,
        ).start()

    def await_bytes(ref, sem):
        pltpu.make_async_copy(ref, ref, sem).wait()

    for copy in loads[: 2 * n_there]:
        copy.wait()
    pl.semaphore_wait(barrier, len(partners))

    for row in there:
        for n, kind, start, width in row:
            for step in (2, 1, 3):
                send(
                    x_buf[n].at[:, 0:TOK],
                    x_buf[n].at[:, pl.ds(step * TOK, TOK)],
                    send_sem.at[1],
                    xa_sem.at[n],
                    (kind, step, 0),
                )

    for copy in loads[2 * n_there : 2 * n_there + 2]:
        copy.wait()
    lane = lax.broadcasted_iota(jnp.int32, (TOK, 128), 1)
    dense = jnp.zeros((TOK, 128), jnp.float32)
    same = (
        lax.broadcasted_iota(jnp.int32, (TOK, TOK), 0) == lax.broadcasted_iota(jnp.int32, (TOK, TOK), 1)
    ).astype(jnp.bfloat16)
    weight = lax.dot_general(same, prob_v[...], NT, preferred_element_type=jnp.float32)
    named = lax.dot_general(
        same, ids_v[...].astype(jnp.bfloat16), NT, preferred_element_type=jnp.float32
    ).astype(jnp.int32)
    for k in range(8):
        dense += jnp.where(named[:, k : k + 1] == lane, weight[:, k : k + 1], 0.0)
    earlier = lax.broadcasted_iota(jnp.int32, (TOK, TOK), 0) > lax.broadcasted_iota(jnp.int32, (TOK, TOK), 1)
    rank = jnp.dot(
        earlier.astype(jnp.bfloat16),
        (dense > 0.0).astype(jnp.bfloat16),
        preferred_element_type=jnp.float32,
    )
    meta = jnp.where(rank > 0.5, -dense, dense).astype(jnp.bfloat16)
    for kind in range(3):
        m_buf[kind][0:TOK] = meta
    for kind in range(3):
        for step in (2, 1, 3):
            rows = pl.ds(step * TOK, TOK)
            send(m_buf[kind].at[0:TOK], m_buf[kind].at[rows], send_sem.at[0], m_sem.at[kind], (kind, step, 0))
    for src, dst, sem in ((w_gate, wg_v, 2), (w_up, wu_v, 3), (w_down, wd_v, 4)):
        load(src.at[0], dst, in_sem.at[sem])

    def as_kind(row, kind):
        z, y, x = (jnp.bitwise_and(lax.shift_right_logical(row, shift), 3) for shift in (6, 3, 1))
        step = (x, y, z)
        moved = step[(kind + 2) % 3] * 64 + step[(kind + 1) % 3] * 8 + step[kind] * 2
        return moved + jnp.bitwise_and(row, 33)

    down = lax.broadcasted_iota(jnp.int32, (256, 256), 0)
    across = lax.broadcasted_iota(jnp.int32, (256, 256), 1)
    for kind in (1, 2):
        to_first[kind - 1][...] = (as_kind(down, kind) == across).astype(jnp.bfloat16)
        from_first[kind - 1][...] = (as_kind(across, kind) == down).astype(jnp.bfloat16)
    for w, row in enumerate(there):
        for n, kind, start, width in row:
            second = (kind + 1) % 3
            if w == 0:
                await_bytes(m_buf[kind].at[TOK : 4 * TOK], m_sem.at[kind])
            await_bytes(x_buf[n].at[:, TOK : 4 * TOK], xa_sem.at[n])
            for step in (2, 1, 3):
                rows = pl.ds(step * 4 * TOK, 4 * TOK)
                if w == 0:
                    send(
                        m_buf[kind].at[0 : 4 * TOK],
                        m_buf[kind].at[rows],
                        send_sem.at[2],
                        m_sem.at[3 + kind],
                        (second, step, 0),
                    )
                if step != 2:
                    send(
                        x_buf[n].at[:, 0 : 4 * TOK],
                        x_buf[n].at[:, rows],
                        send_sem.at[3],
                        xb_sem.at[step // 2, n],
                        (second, step, 0),
                    )

    for row in there:
        for n, kind, start, width in row:
            second = (kind + 1) % 3
            for half, step in ((0, 1), (1, 3)):
                rows = slice(step * 64, step * 64 + 64)
                await_bytes(x_buf[n].at[:, rows], xb_sem.at[half, n])
                send(
                    x_buf[n].at[half, rows],
                    x_buf[n].at[half, 128:192],
                    send_sem.at[8],
                    xb_sem.at[2, n],
                    (second, step, 0),
                )

    def make_tables(kind):
        third = (kind + 2) % 3
        await_bytes(m_buf[kind].at[4 * TOK : 16 * TOK], m_sem.at[3 + kind])
        gathered = m_buf[kind][...]

        def expert(slot):
            block = lax.shift_right_logical(slot, 5)
            step = lax.shift_right_logical(block, 1)
            k = jnp.bitwise_and(core + jnp.bitwise_and(block, 1), 1)
            x, y, z = (jnp.bitwise_and(c + step, 3) if a == third else c for a, c in enumerate(here))
            return (x * 2 + k) * 16 + y * 4 + z

        def table(slot, token, found):
            source = jnp.bitwise_and(lax.shift_right_logical(slot, 1), 15)
            same = source == lax.shift_right_logical(token, 4)
            signed = jnp.where(jnp.bitwise_and(slot, 1) == 1, -found, found)
            return jnp.where(same & (signed > 0.0), signed, 0.0)

        def iota(shape, axis):
            return lax.broadcasted_iota(jnp.int32, shape, axis)

        picks = (iota((128, 256), 0) == expert(iota((128, 256), 1))).astype(jnp.bfloat16)
        found = jnp.dot(gathered, picks, preferred_element_type=jnp.float32)
        q_buf[kind][...] = table(iota((256, 256), 1), iota((256, 256), 0), found).astype(jnp.bfloat16)
        picks = (iota((256, 128), 1) == expert(iota((256, 128), 0))).astype(jnp.bfloat16)
        found = lax.dot_general(picks, gathered, NT, preferred_element_type=jnp.float32)
        taken = table(iota((256, 256), 0), iota((256, 256), 1), found)
        p_buf[kind][...] = (taken > 0.0).astype(jnp.bfloat16)

    def block(step, other):
        return pl.ds((step * 2 + other) * 32, 32)

    exchange = [(2, 0), (2, 1), (1, 0), (3, 0), (1, 1), (3, 1), (0, 1)]

    def landing(w, n, start, width):
        at = start - there[w][0][2]
        return g_buf[w].at[:, :, at : at + width]

    def pack(w, n, kind, start, width):
        third = (kind + 2) % 3
        await_bytes(x_buf[n].at[:, 8 * TOK : 12 * TOK], xb_sem.at[2, n])
        land = landing(w, n, start, width)
        for half in range(2):
            rows = jnp.dot(p_buf[kind][...], x_buf[n][half], preferred_element_type=jnp.float32).astype(jnp.bfloat16)
            land[half, 0:32] = rows[0:32]
            s_buf[n][half] = rows
        for step, other in exchange:
            send(
                s_buf[n].at[:, block(step, other)],
                land.at[:, block(step, other)],
                send_sem.at[4],
                xc_sem.at[n],
                (third, step, other),
            )

    def absorb(w):
        if w == 0:
            for copy in loads[2 * n_there + 2 :]:
                copy.wait()
        for n, kind, start, width in there[w]:
            land = landing(w, n, start, width)
            await_bytes(land.at[:, 32:256], xc_sem.at[n])
            if kind:
                for half in range(2):
                    land[half] = jnp.dot(
                        to_first[kind - 1][...], land[half], preferred_element_type=jnp.float32
                    ).astype(jnp.bfloat16)
        first, span = there[w][0][2], sum(THERE[w]) * TILE

        def columns(cols):
            rows_in, rows_grad = g_buf[w][0], g_buf[w][1]
            gate = jnp.dot(rows_in, wg_v[first : first + span, cols], preferred_element_type=jnp.float32)
            upward = jnp.dot(rows_in, wu_v[first : first + span, cols], preferred_element_type=jnp.float32)
            hidden = lax.dot_general(
                rows_grad, wd_v[cols, first : first + span], NT, preferred_element_type=jnp.float32
            )
            if w > 0:
                gate += gate_acc[:, cols]
                upward += up_acc[:, cols]
                hidden += hid_acc[:, cols]
            return gate, upward, hidden

        def store(i, carry):
            cols = pl.ds(pl.multiple_of(i * N_STEP, N_STEP), N_STEP)
            gate_acc[:, cols], up_acc[:, cols], hid_acc[:, cols] = columns(cols)
            return carry

        if w < len(there) - 1:
            lax.fori_loop(0, F // N_STEP, store, 0)
            return
        for at in range(0, F, LAST_STEP):
            cols = slice(at, at + LAST_STEP)
            gate, upward, hidden = columns(cols)
            s = jax.nn.sigmoid(gate)
            dg_v[0][:, cols] = (hidden * upward * (s * (1.0 + gate * (1.0 - s)))).astype(jnp.bfloat16)
            du_v[0][:, cols] = (hidden * (gate * s)).astype(jnp.bfloat16)

    for w, row in enumerate(there):
        for n, kind, start, width in row:
            if w == 0:
                make_tables(kind)
            pack(w, n, kind, start, width)
        if w >= 1:
            absorb(w - 1)
    absorb(len(there) - 1)

    def reorder(kind):
        order = from_first[kind - 1][...]
        for held in (dg_v, du_v):
            held[kind][...] = jnp.dot(order, held[0][...], preferred_element_type=jnp.float32).astype(jnp.bfloat16)

    def give(n, kind, start, width):
        third = (kind + 2) % 3
        if 0 < n < 3:
            reorder(kind)
        result = lax.dot_general(dg_v[kind][...], wg_v[start : start + width], NT, preferred_element_type=jnp.float32)
        result += lax.dot_general(du_v[kind][...], wu_v[start : start + width], NT, preferred_element_type=jnp.float32)
        result = result.astype(jnp.bfloat16)
        r_buf[n][0:32] = result[0:32]
        b_buf[n][...] = result
        for step, other in exchange:
            send(
                b_buf[n].at[block(step, other)],
                r_buf[n].at[block(step, other)],
                send_sem.at[5],
                rc_sem.at[n],
                (third, (4 - step) % 4, other),
            )

    def combine(n, kind, start, width):
        second = (kind + 1) % 3
        await_bytes(r_buf[n].at[32:256], rc_sem.at[n])
        part = jnp.dot(q_buf[kind][...], r_buf[n][...], preferred_element_type=jnp.float32)
        u_buf[n][...] = part.astype(jnp.bfloat16)
        for step in (2, 1, 3):
            rows = pl.ds(step * 64, 64)
            send(u_buf[n].at[rows], ub_buf[n].at[rows], send_sem.at[6], rb_sem.at[n], (second, 4 - step, 0))

    def reduce_second(n, kind, start, width):
        await_bytes(ub_buf[n].at[64:256], rb_sem.at[n])
        part = u_buf[n][0:64].astype(jnp.float32)
        for step in (1, 2, 3):
            part += ub_buf[n][step * 64 : step * 64 + 64].astype(jnp.float32)
        v_buf[n][...] = part.astype(jnp.bfloat16)
        for step in (2, 1, 3):
            send(
                v_buf[n].at[pl.ds(step * TOK, TOK)],
                va_buf[n].at[pl.ds(step * TOK, TOK)],
                send_sem.at[7],
                ra_sem.at[n],
                (kind, 4 - step, 0),
            )

    def finish(n, kind, start, width):
        await_bytes(va_buf[n].at[TOK : 4 * TOK], ra_sem.at[n])
        part = v_buf[n][0:TOK].astype(jnp.float32)
        for step in (1, 2, 3):
            part += va_buf[n][step * TOK : step * TOK + TOK].astype(jnp.float32)
        out[:, start : start + width] = part

    waves = len(back)
    order = [(give, w) for w in range(waves)]
    for w in range(waves + 2):
        order += [(combine, w), (reduce_second, w - 1), (finish, w - 2)]
    for stage, w in order:
        if 0 <= w < waves:
            for chunk in back[w]:
                stage(*chunk)

    for row in there:
        for n, kind, start, width in row:
            if n < 3:
                await_bytes(m_buf[kind].at[0 : 3 * TOK], send_sem.at[0])
                await_bytes(m_buf[kind].at[0 : 12 * TOK], send_sem.at[2])
            await_bytes(x_buf[n].at[:, 0 : 3 * TOK], send_sem.at[1])
            await_bytes(x_buf[n].at[:, 0 : 8 * TOK], send_sem.at[3])
            await_bytes(x_buf[n].at[:, 0 : 4 * TOK], send_sem.at[8])
            await_bytes(s_buf[n].at[:, 32:256], send_sem.at[4])
    for row in back:
        for n, kind, start, width in row:
            await_bytes(b_buf[n].at[32:256], send_sem.at[5])
            await_bytes(u_buf[n].at[64:256], send_sem.at[6])
            await_bytes(v_buf[n].at[TOK : 4 * TOK], send_sem.at[7])


def local_part(tokens, out_grad, expert_ids, probs, w_gate, w_up, w_down):
    there = [c[3] for row in plan(THERE) for c in row]
    back = [c[3] for row in plan(BACK) for c in row]
    bf16, f32 = jnp.bfloat16, jnp.float32
    scratch = (
        [pltpu.VMEM((2, 256, w), bf16) for _ in range(2) for w in there]
        + [pltpu.VMEM((2, 256, sum(wave) * TILE), bf16) for wave in THERE]
        + [pltpu.VMEM((256, w), bf16) for _ in range(4) for w in back]
        + [pltpu.VMEM((64, w), bf16) for _ in range(2) for w in back]
        + [pltpu.VMEM((256, 128), bf16)] * 3
        + [pltpu.VMEM((256, 256), bf16)] * 10
        + [
            pltpu.VMEM((8, TOK), jnp.int32),
            pltpu.VMEM((8, TOK), bf16),
            pltpu.VMEM((D, F), bf16),
            pltpu.VMEM((D, F), bf16),
            pltpu.VMEM((F, D), bf16),
        ]
        + [pltpu.VMEM((256, F), f32)] * 3
        + [pltpu.VMEM((256, F), bf16)] * 6
        + [
            pltpu.SemaphoreType.DMA((5,)),
            pltpu.SemaphoreType.DMA((2, len(there))),
            pltpu.SemaphoreType.DMA((10,)),
            pltpu.SemaphoreType.DMA((6,)),
            pltpu.SemaphoreType.DMA((len(there),)),
            pltpu.SemaphoreType.DMA((3, len(there))),
            pltpu.SemaphoreType.DMA((len(there),)),
            pltpu.SemaphoreType.DMA((len(back),)),
            pltpu.SemaphoreType.DMA((len(back),)),
            pltpu.SemaphoreType.DMA((len(back),)),
        ]
    )
    total = pl.pallas_call(
        body,
        out_shape=jax.ShapeDtypeStruct((TOK, D), f32),
        in_specs=[pl.BlockSpec(memory_space=pl.ANY)] * 7,
        out_specs=pl.BlockSpec(memory_space=pltpu.VMEM),
        scratch_shapes=scratch,
        compiler_params=pltpu.CompilerParams(
            collective_id=0, has_side_effects=True, vmem_limit_bytes=60 * 1024 * 1024
        ),
        cost_estimate=pl.CostEstimate(flops=2 * 256 * D * F * 5, bytes_accessed=3 * D * F * 2, transcendentals=256 * F),
    )(tokens, out_grad, expert_ids.T, probs.T, w_gate, w_up, w_down)
    return total.astype(bf16)


def solution(mesh):
    flat = P(("group", "local"), None)
    deep = P(("group", "local"), None, None)
    return jax.shard_map(
        local_part,
        mesh=mesh,
        in_specs=(flat, flat, flat, flat, deep, deep, deep),
        out_specs=flat,
        check_vma=False,
    )
```

```python
import jax
import jax.numpy as jnp
from jax import lax
from jax.experimental import pallas as pl
from jax.experimental.pallas import tpu as pltpu
from jax.sharding import PartitionSpec as P

MESH = pl.DeviceIdType.MESH
D = 3584
F = 1024
TOK = 16
TILE = 128
THERE = ((4, 4, 4), (4, 3, 3), (2, 2, 2))
BACK = ((4, 4, 4), (4, 3, 3), (2, 2, 2))
N_STEP = 1024
LAST_STEP = 512
NT = (((1,), (1,)), ((), ()))


def plan(waves):
    chunks, start = [], 0
    for wave in waves:
        row = []
        for kind, tiles in enumerate(wave):
            row.append((len(chunks) * 3 + kind, kind, start * TILE, tiles * TILE))
            start += tiles
        chunks.append(row)
    return chunks


def body(tokens, grads, ids, probs, w_gate, w_up, w_down, out, *scratch):
    there, back = plan(THERE), plan(BACK)
    n_there, n_back = 3 * len(THERE), 3 * len(BACK)
    scratch = list(scratch)

    def take(count):
        taken = scratch[:count]
        del scratch[:count]
        return taken

    x_buf, s_buf, g_buf = take(n_there), take(n_there), take(len(THERE))
    b_buf, r_buf, u_buf, ub_buf, v_buf, va_buf = (take(n_back) for _ in range(6))
    m_buf = take(3)
    p_buf, q_buf = take(3), take(3)
    to_first, from_first = take(2), take(2)
    ids_v, prob_v, wg_v, wu_v, wd_v = take(5)
    gate_acc, up_acc, hid_acc = take(3)
    dg_v, du_v = take(3), take(3)
    in_sem, x_sem, send_sem, m_sem, xa_sem, xb_sem, xc_sem, rc_sem, rb_sem, ra_sem = take(10)

    group, local = lax.axis_index("group"), lax.axis_index("local")
    here = (group // 2, local // 4, local % 4)
    core = group % 2

    def device(axis, step, other):
        x, y, z = (lax.rem(c + (step if a == axis else 0), 4) for a, c in enumerate(here))
        k = lax.rem(core + other, 2)
        return (x * 2 + k, y * 4 + z)

    partners = [(axis, step, other) for axis in range(3) for step in (1, 2, 3) for other in (0, 1)]
    partners.append((0, 0, 1))
    barrier = pltpu.get_barrier_semaphore()
    for partner in partners:
        pl.semaphore_signal(barrier, inc=1, device_id=device(*partner), device_id_type=MESH)

    loads = []

    def load(src, dst, sem):
        loads.append(pltpu.make_async_copy(src, dst, sem))
        loads[-1].start()

    for row in there:
        for n, kind, start, width in row:
            cols = slice(start, start + width)
            load(tokens.at[:, cols], x_buf[n].at[0, 0:TOK], x_sem.at[0, n])
            load(grads.at[:, cols], x_buf[n].at[1, 0:TOK], x_sem.at[1, n])
    load(ids, ids_v, in_sem.at[0])
    load(probs, prob_v, in_sem.at[1])

    def send(src, dst, sem, recv, target):
        pltpu.make_async_remote_copy(
            src_ref=src,
            dst_ref=dst,
            send_sem=sem,
            recv_sem=recv,
            device_id=device(*target),
            device_id_type=MESH,
        ).start()

    def await_bytes(ref, sem):
        pltpu.make_async_copy(ref, ref, sem).wait()

    for copy in loads[: 2 * n_there]:
        copy.wait()
    pl.semaphore_wait(barrier, len(partners))

    for row in there:
        for n, kind, start, width in row:
            for step in (2, 1, 3):
                send(
                    x_buf[n].at[:, 0:TOK],
                    x_buf[n].at[:, pl.ds(step * TOK, TOK)],
                    send_sem.at[1],
                    xa_sem.at[n],
                    (kind, step, 0),
                )

    for copy in loads[2 * n_there : 2 * n_there + 2]:
        copy.wait()
    lane = lax.broadcasted_iota(jnp.int32, (TOK, 128), 1)
    dense = jnp.zeros((TOK, 128), jnp.float32)
    same = (
        lax.broadcasted_iota(jnp.int32, (TOK, TOK), 0) == lax.broadcasted_iota(jnp.int32, (TOK, TOK), 1)
    ).astype(jnp.bfloat16)
    weight = lax.dot_general(same, prob_v[...], NT, preferred_element_type=jnp.float32)
    named = lax.dot_general(
        same, ids_v[...].astype(jnp.bfloat16), NT, preferred_element_type=jnp.float32
    ).astype(jnp.int32)
    for k in range(8):
        dense += jnp.where(named[:, k : k + 1] == lane, weight[:, k : k + 1], 0.0)
    earlier = lax.broadcasted_iota(jnp.int32, (TOK, TOK), 0) > lax.broadcasted_iota(jnp.int32, (TOK, TOK), 1)
    rank = jnp.dot(
        earlier.astype(jnp.bfloat16),
        (dense > 0.0).astype(jnp.bfloat16),
        preferred_element_type=jnp.float32,
    )
    meta = jnp.where(rank > 0.5, -dense, dense).astype(jnp.bfloat16)
    for kind in range(3):
        m_buf[kind][0:TOK] = meta
    for kind in range(3):
        for step in (2, 1, 3):
            rows = pl.ds(step * TOK, TOK)
            send(m_buf[kind].at[0:TOK], m_buf[kind].at[rows], send_sem.at[0], m_sem.at[kind], (kind, step, 0))
    for src, dst, sem in ((w_gate, wg_v, 2), (w_up, wu_v, 3), (w_down, wd_v, 4)):
        load(src.at[0], dst, in_sem.at[sem])

    def as_kind(row, kind):
        z, y, x = (jnp.bitwise_and(lax.shift_right_logical(row, shift), 3) for shift in (6, 3, 1))
        step = (x, y, z)
        moved = step[(kind + 2) % 3] * 64 + step[(kind + 1) % 3] * 8 + step[kind] * 2
        return moved + jnp.bitwise_and(row, 33)

    down = lax.broadcasted_iota(jnp.int32, (256, 256), 0)
    across = lax.broadcasted_iota(jnp.int32, (256, 256), 1)
    for kind in (1, 2):
        to_first[kind - 1][...] = (as_kind(down, kind) == across).astype(jnp.bfloat16)
        from_first[kind - 1][...] = (as_kind(across, kind) == down).astype(jnp.bfloat16)
    for w, row in enumerate(there):
        for n, kind, start, width in row:
            second = (kind + 1) % 3
            if w == 0:
                await_bytes(m_buf[kind].at[TOK : 4 * TOK], m_sem.at[kind])
            await_bytes(x_buf[n].at[:, TOK : 4 * TOK], xa_sem.at[n])
            for step in (2, 1, 3):
                rows = pl.ds(step * 4 * TOK, 4 * TOK)
                if w == 0:
                    send(
                        m_buf[kind].at[0 : 4 * TOK],
                        m_buf[kind].at[rows],
                        send_sem.at[2],
                        m_sem.at[3 + kind],
                        (second, step, 0),
                    )
                if step != 2:
                    send(
                        x_buf[n].at[:, 0 : 4 * TOK],
                        x_buf[n].at[:, rows],
                        send_sem.at[3],
                        xb_sem.at[step // 2, n],
                        (second, step, 0),
                    )

    for row in there:
        for n, kind, start, width in row:
            second = (kind + 1) % 3
            for half, step in ((0, 1), (1, 3)):
                rows = slice(step * 64, step * 64 + 64)
                await_bytes(x_buf[n].at[:, rows], xb_sem.at[half, n])
                send(
                    x_buf[n].at[half, rows],
                    x_buf[n].at[half, 128:192],
                    send_sem.at[8],
                    xb_sem.at[2, n],
                    (second, step, 0),
                )

    def make_tables(kind):
        third = (kind + 2) % 3
        await_bytes(m_buf[kind].at[4 * TOK : 16 * TOK], m_sem.at[3 + kind])
        gathered = m_buf[kind][...]

        def expert(slot):
            block = lax.shift_right_logical(slot, 5)
            step = lax.shift_right_logical(block, 1)
            k = jnp.bitwise_and(core + jnp.bitwise_and(block, 1), 1)
            x, y, z = (jnp.bitwise_and(c + step, 3) if a == third else c for a, c in enumerate(here))
            return (x * 2 + k) * 16 + y * 4 + z

        def table(slot, token, found):
            source = jnp.bitwise_and(lax.shift_right_logical(slot, 1), 15)
            same = source == lax.shift_right_logical(token, 4)
            signed = jnp.where(jnp.bitwise_and(slot, 1) == 1, -found, found)
            return jnp.where(same & (signed > 0.0), signed, 0.0)

        def iota(shape, axis):
            return lax.broadcasted_iota(jnp.int32, shape, axis)

        picks = (iota((128, 256), 0) == expert(iota((128, 256), 1))).astype(jnp.bfloat16)
        found = jnp.dot(gathered, picks, preferred_element_type=jnp.float32)
        q_buf[kind][...] = table(iota((256, 256), 1), iota((256, 256), 0), found).astype(jnp.bfloat16)
        picks = (iota((256, 128), 1) == expert(iota((256, 128), 0))).astype(jnp.bfloat16)
        found = lax.dot_general(picks, gathered, NT, preferred_element_type=jnp.float32)
        taken = table(iota((256, 256), 0), iota((256, 256), 1), found)
        p_buf[kind][...] = (taken > 0.0).astype(jnp.bfloat16)

    def block(step, other):
        return pl.ds((step * 2 + other) * 32, 32)

    exchange = [(2, 0), (2, 1), (1, 0), (3, 0), (1, 1), (3, 1), (0, 1)]

    def landing(w, n, start, width):
        at = start - there[w][0][2]
        return g_buf[w].at[:, :, at : at + width]

    def pack(w, n, kind, start, width):
        third = (kind + 2) % 3
        await_bytes(x_buf[n].at[:, 8 * TOK : 12 * TOK], xb_sem.at[2, n])
        land = landing(w, n, start, width)
        for half in range(2):
            rows = jnp.dot(p_buf[kind][...], x_buf[n][half], preferred_element_type=jnp.float32).astype(jnp.bfloat16)
            land[half, 0:32] = rows[0:32]
            s_buf[n][half] = rows
        for step, other in exchange:
            send(
                s_buf[n].at[:, block(step, other)],
                land.at[:, block(step, other)],
                send_sem.at[4],
                xc_sem.at[n],
                (third, step, other),
            )

    def absorb(w):
        if w == 0:
            for copy in loads[2 * n_there + 2 :]:
                copy.wait()
        for n, kind, start, width in there[w]:
            land = landing(w, n, start, width)
            await_bytes(land.at[:, 32:256], xc_sem.at[n])
            if kind:
                for half in range(2):
                    land[half] = jnp.dot(
                        to_first[kind - 1][...], land[half], preferred_element_type=jnp.float32
                    ).astype(jnp.bfloat16)
        first, span = there[w][0][2], sum(THERE[w]) * TILE

        def columns(cols):
            rows_in, rows_grad = g_buf[w][0], g_buf[w][1]
            gate = jnp.dot(rows_in, wg_v[first : first + span, cols], preferred_element_type=jnp.float32)
            upward = jnp.dot(rows_in, wu_v[first : first + span, cols], preferred_element_type=jnp.float32)
            hidden = lax.dot_general(
                rows_grad, wd_v[cols, first : first + span], NT, preferred_element_type=jnp.float32
            )
            if w > 0:
                gate += gate_acc[:, cols]
                upward += up_acc[:, cols]
                hidden += hid_acc[:, cols]
            return gate, upward, hidden

        def store(i, carry):
            cols = pl.ds(pl.multiple_of(i * N_STEP, N_STEP), N_STEP)
            gate_acc[:, cols], up_acc[:, cols], hid_acc[:, cols] = columns(cols)
            return carry

        if w < len(there) - 1:
            lax.fori_loop(0, F // N_STEP, store, 0)
            return
        for at in range(0, F, LAST_STEP):
            cols = slice(at, at + LAST_STEP)
            gate, upward, hidden = columns(cols)
            s = jax.nn.sigmoid(gate)
            dg_v[0][:, cols] = (hidden * upward * (s * (1.0 + gate * (1.0 - s)))).astype(jnp.bfloat16)
            du_v[0][:, cols] = (hidden * (gate * s)).astype(jnp.bfloat16)

    for w, row in enumerate(there):
        for n, kind, start, width in row:
            if w == 0:
                make_tables(kind)
            pack(w, n, kind, start, width)
        if w >= 1:
            absorb(w - 1)
    absorb(len(there) - 1)

    def reorder(kind):
        order = from_first[kind - 1][...]
        for held in (dg_v, du_v):
            held[kind][...] = jnp.dot(order, held[0][...], preferred_element_type=jnp.float32).astype(jnp.bfloat16)

    def give(n, kind, start, width):
        third = (kind + 2) % 3
        if 0 < n < 3:
            reorder(kind)
        result = lax.dot_general(dg_v[kind][...], wg_v[start : start + width], NT, preferred_element_type=jnp.float32)
        result += lax.dot_general(du_v[kind][...], wu_v[start : start + width], NT, preferred_element_type=jnp.float32)
        result = result.astype(jnp.bfloat16)
        r_buf[n][0:32] = result[0:32]
        b_buf[n][...] = result
        for step, other in exchange:
            send(
                b_buf[n].at[block(step, other)],
                r_buf[n].at[block(step, other)],
                send_sem.at[5],
                rc_sem.at[n],
                (third, (4 - step) % 4, other),
            )

    def combine(n, kind, start, width):
        second = (kind + 1) % 3
        await_bytes(r_buf[n].at[32:256], rc_sem.at[n])
        part = jnp.dot(q_buf[kind][...], r_buf[n][...], preferred_element_type=jnp.float32)
        u_buf[n][...] = part.astype(jnp.bfloat16)
        for step in (2, 1, 3):
            rows = pl.ds(step * 64, 64)
            send(u_buf[n].at[rows], ub_buf[n].at[rows], send_sem.at[6], rb_sem.at[n], (second, 4 - step, 0))

    def reduce_second(n, kind, start, width):
        await_bytes(ub_buf[n].at[64:256], rb_sem.at[n])
        part = u_buf[n][0:64].astype(jnp.float32)
        for step in (1, 2, 3):
            part += ub_buf[n][step * 64 : step * 64 + 64].astype(jnp.float32)
        v_buf[n][...] = part.astype(jnp.bfloat16)
        for step in (2, 1, 3):
            send(
                v_buf[n].at[pl.ds(step * TOK, TOK)],
                va_buf[n].at[pl.ds(step * TOK, TOK)],
                send_sem.at[7],
                ra_sem.at[n],
                (kind, 4 - step, 0),
            )

    def finish(n, kind, start, width):
        await_bytes(va_buf[n].at[TOK : 4 * TOK], ra_sem.at[n])
        part = v_buf[n][0:TOK].astype(jnp.float32)
        for step in (1, 2, 3):
            part += va_buf[n][step * TOK : step * TOK + TOK].astype(jnp.float32)
        out[:, start : start + width] = part

    waves = len(back)
    order = [(give, w) for w in range(waves)]
    for stage in (combine, reduce_second, finish):
        order += [(stage, w) for w in range(waves)]
    for stage, w in order:
        if 0 <= w < waves:
            for chunk in back[w]:
                stage(*chunk)

    for row in there:
        for n, kind, start, width in row:
            if n < 3:
                await_bytes(m_buf[kind].at[0 : 3 * TOK], send_sem.at[0])
                await_bytes(m_buf[kind].at[0 : 12 * TOK], send_sem.at[2])
            await_bytes(x_buf[n].at[:, 0 : 3 * TOK], send_sem.at[1])
            await_bytes(x_buf[n].at[:, 0 : 8 * TOK], send_sem.at[3])
            await_bytes(x_buf[n].at[:, 0 : 4 * TOK], send_sem.at[8])
            await_bytes(s_buf[n].at[:, 32:256], send_sem.at[4])
    for row in back:
        for n, kind, start, width in row:
            await_bytes(b_buf[n].at[32:256], send_sem.at[5])
            await_bytes(u_buf[n].at[64:256], send_sem.at[6])
            await_bytes(v_buf[n].at[TOK : 4 * TOK], send_sem.at[7])


def local_part(tokens, out_grad, expert_ids, probs, w_gate, w_up, w_down):
    there = [c[3] for row in plan(THERE) for c in row]
    back = [c[3] for row in plan(BACK) for c in row]
    bf16, f32 = jnp.bfloat16, jnp.float32
    scratch = (
        [pltpu.VMEM((2, 256, w), bf16) for _ in range(2) for w in there]
        + [pltpu.VMEM((2, 256, sum(wave) * TILE), bf16) for wave in THERE]
        + [pltpu.VMEM((256, w), bf16) for _ in range(4) for w in back]
        + [pltpu.VMEM((64, w), bf16) for _ in range(2) for w in back]
        + [pltpu.VMEM((256, 128), bf16)] * 3
        + [pltpu.VMEM((256, 256), bf16)] * 10
        + [
            pltpu.VMEM((8, TOK), jnp.int32),
            pltpu.VMEM((8, TOK), bf16),
            pltpu.VMEM((D, F), bf16),
            pltpu.VMEM((D, F), bf16),
            pltpu.VMEM((F, D), bf16),
        ]
        + [pltpu.VMEM((256, F), f32)] * 3
        + [pltpu.VMEM((256, F), bf16)] * 6
        + [
            pltpu.SemaphoreType.DMA((5,)),
            pltpu.SemaphoreType.DMA((2, len(there))),
            pltpu.SemaphoreType.DMA((10,)),
            pltpu.SemaphoreType.DMA((6,)),
            pltpu.SemaphoreType.DMA((len(there),)),
            pltpu.SemaphoreType.DMA((3, len(there))),
            pltpu.SemaphoreType.DMA((len(there),)),
            pltpu.SemaphoreType.DMA((len(back),)),
            pltpu.SemaphoreType.DMA((len(back),)),
            pltpu.SemaphoreType.DMA((len(back),)),
        ]
    )
    total = pl.pallas_call(
        body,
        out_shape=jax.ShapeDtypeStruct((TOK, D), f32),
        in_specs=[pl.BlockSpec(memory_space=pl.ANY)] * 7,
        out_specs=pl.BlockSpec(memory_space=pltpu.VMEM),
        scratch_shapes=scratch,
        compiler_params=pltpu.CompilerParams(
            collective_id=0, has_side_effects=True, vmem_limit_bytes=60 * 1024 * 1024
        ),
        cost_estimate=pl.CostEstimate(flops=2 * 256 * D * F * 5, bytes_accessed=3 * D * F * 2, transcendentals=256 * F),
    )(tokens, out_grad, expert_ids.T, probs.T, w_gate, w_up, w_down)
    return total.astype(bf16)


def solution(mesh):
    flat = P(("group", "local"), None)
    deep = P(("group", "local"), None, None)
    return jax.shard_map(
        local_part,
        mesh=mesh,
        in_specs=(flat, flat, flat, flat, deep, deep, deep),
        out_specs=flat,
        check_vma=False,
    )
```
